32 devices in a mesh: tm: 4 (over y, x), row: 8 (over z, core).
Axes of the slice: x: 2, y: 2, z: 4, core: 2. Of those that a mesh axis runs over, the one named last changes fastest.
Arguments:
- video_clip: bfloat16 [64, 64, 64, 128], P('tm', 'row'), may hold values from -6 to 6
- spatial_one: bfloat16 [3, 3, 144, 64], replicated, may hold values from -0.25 to 0.25
- temporal_one: bfloat16 [3, 64, 144], replicated, may hold values from -0.3125 to 0.3125
- down_weight: bfloat16 [3, 3, 128, 64], replicated, may hold values from -0.25 to 0.25
- spatial_two: bfloat16 [3, 3, 288, 128], replicated, may hold values from -0.1875 to 0.1875
- temporal_two: bfloat16 [3, 128, 288], replicated, may hold values from -0.21875 to 0.21875
Outputs:
- encoded: bfloat16 [64, 32, 64, 128], P('tm', 'row')
The draws below stay inside these ranges and needn't reach their ends.
All inputs are finite; a program needn't handle non-finite values.
Results may differ from the reference program's by a relative error of at most 0.0061.
Values may be sent and summed in bfloat16 or wider, within the bound.
A program may use at most 64 MiB of HBM per device.

```python
import jax
import jax.numpy as jnp
from jax import lax

C1 = 64
M1 = 144
C2 = 128
M2 = 288
WIDTH = 128
FRAMES = 64
HEIGHT = 64


def levels(own_key, shape, split, low, largest):
    def one(position, parts):
        steps = jax.random.uniform(jax.random.fold_in(jax.random.fold_in(own_key, 6), position), (parts,), jnp.float32, low / len(split), largest / len(split))
        return jnp.repeat(jnp.exp(steps), shape[position] // parts).reshape((-1,) + (1,) * (len(shape) - position - 1))

    loudness = one(*split[0])
    for cut in split[1:]:
        loudness = loudness * one(*cut)
    return loudness


def scatter_about(own_key, dims, scale, most, split=(), held_as=jnp.bfloat16):
    drawn = jax.random.normal(own_key, dims, jnp.float32) * scale
    if len(split) > 0:
        drawn = levels(own_key, dims, split, -0.22, 0.18) * drawn
    return jnp.clip(drawn, min=-most, max=most).astype(held_as)


def setup_inputs(seed: int = 0) -> dict:
    arg_keys = jax.random.split(jax.random.key(seed), 7)
    return {
        "video_clip": scatter_about(arg_keys[0], (FRAMES, HEIGHT, C1, WIDTH), 1.0, 6.0, ((0, 4), (1, 8))),
        "spatial_one": scatter_about(arg_keys[1], (3, 3, M1, C1), (9 * C1) ** -0.5, 0.25),
        "temporal_one": scatter_about(arg_keys[2], (3, C1, M1), (3 * M1) ** -0.5, 0.3125),
        "down_weight": scatter_about(arg_keys[3], (3, 3, C2, C1), (9 * C1) ** -0.5, 0.25),
        "spatial_two": scatter_about(arg_keys[4], (3, 3, M2, C2), (9 * C2) ** -0.5, 0.1875),
        "temporal_two": scatter_about(arg_keys[5], (3, C2, M2), (3 * M2) ** -0.5, 0.21875),
    }


def spatial(source, kernel, layout, margin, strides):
    return lax.conv_general_dilated(source, kernel, strides, ((margin, margin), (1, 1)), dimension_numbers=(layout, "HWOI", layout), preferred_element_type=jnp.float32)


def temporal(source, kernel, layout, margin):
    return lax.conv_general_dilated(source, kernel[:, None], (1, 1), ((margin, margin), (0, 0)), dimension_numbers=(layout, "HWOI", layout), preferred_element_type=jnp.float32)


def reference(video_clip, spatial_one, temporal_one, down_weight, spatial_two, temporal_two):
    middle_one = jax.nn.relu(spatial(video_clip, spatial_one, "NHCW", 1, (1, 1))).astype(jnp.bfloat16)
    section_one = jax.nn.relu(video_clip.astype(jnp.float32) + temporal(middle_one, temporal_one, "HWCN", 1)).astype(jnp.bfloat16)
    reduced = lax.conv_general_dilated(section_one, down_weight, (2, 2), ((1, 1), (1, 1)), dimension_numbers=("NHCW", "HWOI", "NHWC"), preferred_element_type=jnp.float32)
    reduced = jax.nn.relu(reduced).astype(jnp.bfloat16)
    middle_two = jax.nn.relu(spatial(reduced, spatial_two, "NHWC", 1, (1, 1))).astype(jnp.bfloat16)
    encoded = jax.nn.relu(reduced.astype(jnp.float32) + temporal(middle_two, temporal_two, "HWNC", 1)).astype(jnp.bfloat16)
    return encoded
```

```python
import functools

import jax
import jax.numpy as jnp
from jax import lax
from jax.experimental import pallas as pl
from jax.experimental.pallas import tpu as pltpu
from jax.sharding import PartitionSpec as P

MESH = pl.DeviceIdType.MESH
SIDES = [(dt, dr) for dt in (-1, 0, 1) for dr in (-1, 0, 1) if (dt, dr) != (0, 0)]
BF16 = jnp.bfloat16
F32 = jnp.float32


def span(step, size, low, high):
    if step == 0:
        return 0, low, size
    if step == 1:
        return size - low, 0, low
    return 0, low + size, high


def halo_kernel(tms, rows, low, high, x_ref, p_ref, own_sem, send_sem, recv_sem):
    tm, row = lax.axis_index("tm"), lax.axis_index("row")
    frames, height = x_ref.shape[:2]
    own = pltpu.make_async_copy(
        x_ref, p_ref.at[pl.ds(1, frames), pl.ds(low, height)], own_sem
    )
    own.start()

    def there(dt, dr):
        t, r = tm + dt, row + dr
        return (t >= 0) & (t < tms) & (r >= 0) & (r < rows)

    barrier = pltpu.get_barrier_semaphore()
    for dt, dr in SIDES:

        @pl.when(there(dt, dr))
        def _():
            pl.semaphore_signal(
                barrier, inc=1, device_id=(tm + dt, row + dr), device_id_type=MESH
            )

    peers = sum(there(dt, dr).astype(jnp.int32) for dt, dr in SIDES)
    pl.semaphore_wait(barrier, peers)

    def copy(k):
        dt, dr = SIDES[k]
        t_from, t_to, t_len = span(dt, frames, 1, 1)
        r_from, r_to, r_len = span(dr, height, low, high)
        return pltpu.make_async_remote_copy(
            src_ref=x_ref.at[pl.ds(t_from, t_len), pl.ds(r_from, r_len)],
            dst_ref=p_ref.at[pl.ds(t_to, t_len), pl.ds(r_to, r_len)],
            send_sem=send_sem.at[k],
            recv_sem=recv_sem.at[k],
            device_id=(tm + dt, row + dr),
            device_id_type=MESH,
        )

    for k, (dt, dr) in enumerate(SIDES):

        @pl.when(there(dt, dr))
        def _():
            copy(k).start()

    for k, (dt, dr) in enumerate(SIDES):
        _, t_to, t_len = span(dt, frames, 1, 1)
        _, r_to, r_len = span(dr, height, low, high)

        @pl.when(jnp.logical_not(there(-dt, -dr)))
        def _():
            def clear(t, carry):
                p_ref[t_to + t, r_to : r_to + r_len] = jnp.zeros(
                    (r_len,) + p_ref.shape[2:], p_ref.dtype
                )
                return carry

            lax.fori_loop(0, t_len, clear, 0)

    for k, (dt, dr) in enumerate(SIDES):

        @pl.when(there(-dt, -dr))
        def _():
            copy(k).wait_recv()

        @pl.when(there(dt, dr))
        def _():
            copy(k).wait_send()

    own.wait()


def halo(x, mesh, low, high, collective_id):
    frames, height = x.shape[:2]
    return pl.pallas_call(
        functools.partial(halo_kernel, mesh.shape["tm"], mesh.shape["row"], low, high),
        out_shape=jax.ShapeDtypeStruct((frames + 2, height + low + high) + x.shape[2:], x.dtype),
        in_specs=[pl.BlockSpec(memory_space=pltpu.VMEM)],
        out_specs=pl.BlockSpec(memory_space=pltpu.VMEM),
        scratch_shapes=[
            pltpu.SemaphoreType.DMA,
            pltpu.SemaphoreType.DMA((len(SIDES),)),
            pltpu.SemaphoreType.DMA((len(SIDES),)),
        ],
        compiler_params=pltpu.CompilerParams(
            collective_id=collective_id, has_side_effects=True, vmem_limit_bytes=32 << 20
        ),
        name="halo",
    )(x)


def nt(a, b):
    return lax.dot_general(a, b, (((1,), (1,)), ((), ())), preferred_element_type=F32)


def shifted(x, axis):
    size = x.shape[axis]
    wide = x.astype(F32)
    place = lax.broadcasted_iota(jnp.int32, x.shape, axis)
    before = jnp.where(place == 0, 0.0, pltpu.roll(wide, 1, axis)).astype(BF16)
    after = jnp.where(place == size - 1, 0.0, pltpu.roll(wide, size - 1, axis)).astype(BF16)
    return before, after


def first_kernel(p_ref, w1_ref, t1_ref, d_ref, out_ref, w_s, col_s, z_s, s_s, g_s):
    frames, height = out_ref.shape[0], p_ref.shape[1] - 3
    c1, width = p_ref.shape[2:]
    m1 = w1_ref.shape[3]
    half = width // 2
    kept = height + 1
    for a in range(3):
        for b in range(3):
            k = (3 * a + b) * c1
            w_s[:, k : k + c1] = w1_ref[a, b].T
    taps = t1_ref[...].reshape(3 * c1, m1)

    def spatial_pair(pair, carry):
        for r in range(height + 3):
            for f in range(2):
                x = p_ref[2 * pair + f, r]
                before, after = shifted(x, 1)
                lanes = slice(f * width, (f + 1) * width)
                k = 3 * c1 * r
                col_s[k : k + c1, lanes] = before
                col_s[k + c1 : k + 2 * c1, lanes] = x
                col_s[k + 2 * c1 : k + 3 * c1, lanes] = after
        for h in range(kept):
            col = col_s[3 * c1 * h : 3 * c1 * (h + 3), :]
            middle = jnp.dot(w_s[...], col, preferred_element_type=F32)
            middle = jnp.maximum(middle, 0.0).astype(BF16)
            z = jnp.dot(taps, middle, preferred_element_type=F32)
            z_s[2 * pair, h] = z[:, :width]
            z_s[2 * pair + 1, h] = z[:, width:]
        return carry

    lax.fori_loop(0, (frames + 2) // 2, spatial_pair, 0)

    top = jnp.where(lax.axis_index("row") == 0, 0.0, 1.0)
    tap = lax.broadcasted_iota(jnp.int32, (3 * half, width), 0)
    column = lax.broadcasted_iota(jnp.int32, (3 * half, width), 1)
    pick = column == 2 * lax.rem(tap, half) + tap // half - 1
    pick = jnp.where(pick, 1.0, 0.0).astype(BF16)

    def section(f, carry):
        for h in range(kept):
            s = p_ref[f + 1, h + 1].astype(F32) + z_s[f, h, :c1]
            s = s + z_s[f + 1, h, c1 : 2 * c1] + z_s[f + 2, h, 2 * c1 :]
            s = jnp.maximum(s, 0.0)
            if h == 0:
                s = s * top
            s_s[h * c1 : (h + 1) * c1, :] = s.astype(BF16)
        g = nt(pick, s_s[...]).astype(BF16)
        rows = pl.ds(pl.multiple_of(f * half, half), half)
        for b in range(3):
            g_s[b, rows, :] = g[b * half : (b + 1) * half]
        return carry

    lax.fori_loop(0, frames, section, 0)

    group = 4

    def down(q, carry):
        rows = pl.ds(pl.multiple_of(q * group * half, group * half), group * half)
        for i in range(height // 2):
            total = None
            for b in range(3):
                lhs = g_s[b, rows, 2 * c1 * i : 2 * c1 * i + 3 * c1]
                rhs = jnp.concatenate([d_ref[a, b] for a in range(3)], axis=0)
                part = jnp.dot(lhs, rhs, preferred_element_type=F32)
                total = part if total is None else total + part
            total = jnp.maximum(total, 0.0).astype(BF16)
            out_ref[pl.ds(q * group, group), i] = total.reshape(group, half, total.shape[1])
        return carry

    lax.fori_loop(0, frames // group, down, 0)


def first(padded, spatial_one, temporal_one, down_weight):
    frames, height = padded.shape[0] - 2, padded.shape[1] - 3
    c1, width = padded.shape[2:]
    m1, c2 = spatial_one.shape[3], down_weight.shape[3]
    kept = height + 1
    vmem = pl.BlockSpec(memory_space=pltpu.VMEM)
    return pl.pallas_call(
        first_kernel,
        out_shape=jax.ShapeDtypeStruct((frames, height // 2, width // 2, c2), BF16),
        in_specs=[vmem] * 4,
        out_specs=vmem,
        scratch_shapes=[
            pltpu.VMEM((m1, 9 * c1), BF16),
            pltpu.VMEM((3 * c1 * (height + 3), 2 * width), BF16),
            pltpu.VMEM((frames + 2, kept, 3 * c1, width), F32),
            pltpu.VMEM((kept * c1, width), BF16),
            pltpu.VMEM((3, frames * width // 2, kept * c1), BF16),
        ],
        compiler_params=pltpu.CompilerParams(vmem_limit_bytes=48 << 20),
        name="first",
    )(padded, spatial_one, temporal_one, down_weight)


def second_kernel(p_ref, w2_ref, t2_ref, out_ref, w_s, v_s, m_s):
    frames, height = out_ref.shape[:2]
    width, c2 = p_ref.shape[2:]
    for a in range(3):
        for b in range(3):
            k = (3 * a + b) * c2
            w_s[k : k + c2, :] = w2_ref[a, b].T

    def columns(t, carry):
        rows = pl.ds(pl.multiple_of(t * width, width), width)
        for i in range(height + 2):
            x = p_ref[t, i]
            before, after = shifted(x, 0)
            v_s[i, rows, :c2] = before
            v_s[i, rows, c2 : 2 * c2] = x
            v_s[i, rows, 2 * c2 :] = after
        return carry

    lax.fori_loop(0, frames + 2, columns, 0)

    group = 3

    def spatial(q, carry):
        rows = pl.ds(pl.multiple_of(q * group * width, group * width), group * width)
        for i in range(height):
            lhs = jnp.concatenate([v_s[i + a, rows, :] for a in range(3)], axis=1)
            middle = jnp.dot(lhs, w_s[...], preferred_element_type=F32)
            m_s[i, rows, :] = jnp.maximum(middle, 0.0).astype(BF16)
        return carry

    lax.fori_loop(0, (frames + 2) // group, spatial, 0)

    span_t = 4

    def temporal(q, carry):
        for i in range(height):
            total = p_ref[pl.ds(q * span_t + 1, span_t), i + 1].astype(F32)
            total = total.reshape(span_t * width, c2)
            for k in range(3):
                start = pl.multiple_of((q * span_t + k) * width, width)
                lhs = m_s[i, pl.ds(start, span_t * width), :]
                total = total + jnp.dot(lhs, t2_ref[k], preferred_element_type=F32)
            total = jnp.maximum(total, 0.0).astype(BF16)
            out_ref[pl.ds(q * span_t, span_t), i] = total.reshape(span_t, width, c2)
        return carry

    lax.fori_loop(0, frames // span_t, temporal, 0)


def second(padded, spatial_two, temporal_two):
    frames, height = padded.shape[0] - 2, padded.shape[1] - 2
    width, c2 = padded.shape[2:]
    m2 = spatial_two.shape[2]
    vmem = pl.BlockSpec(memory_space=pltpu.VMEM)
    return pl.pallas_call(
        second_kernel,
        out_shape=jax.ShapeDtypeStruct((frames, height, width, c2), BF16),
        in_specs=[vmem] * 3,
        out_specs=vmem,
        scratch_shapes=[
            pltpu.VMEM((9 * c2, m2), BF16),
            pltpu.VMEM((height + 2, (frames + 2) * width, 3 * c2), BF16),
            pltpu.VMEM((height, (frames + 2) * width, m2), BF16),
        ],
        compiler_params=pltpu.CompilerParams(vmem_limit_bytes=48 << 20),
        name="second",
    )(padded, spatial_two, temporal_two)


def on_device(mesh, video_clip, spatial_one, temporal_one, down_weight, spatial_two, temporal_two):
    down = jnp.transpose(down_weight, (0, 1, 3, 2))
    one = jnp.transpose(spatial_one, (0, 1, 3, 2))
    temporal = jnp.transpose(temporal_two, (0, 2, 1))
    padded = halo(video_clip, mesh, 2, 1, 0)
    reduced = first(padded, one, temporal_one, down)
    padded = halo(reduced, mesh, 1, 1, 1)
    return second(padded, spatial_two, temporal)


def solution(mesh):
    placed = (P("tm", "row", None, None), P(), P(), P(), P(), P())
    return jax.shard_map(
        functools.partial(on_device, mesh),
        mesh=mesh,
        in_specs=placed,
        out_specs=P("tm", "row", None, None),
        check_vma=False,
    )
```

```python
import functools

import jax
import jax.numpy as jnp
from jax import lax
from jax.experimental import pallas as pl
from jax.experimental.pallas import tpu as pltpu
from jax.sharding import PartitionSpec as P

MESH = pl.DeviceIdType.MESH
SIDES = [(dt, dr) for dt in (-1, 0, 1) for dr in (-1, 0, 1) if (dt, dr) != (0, 0)]
BF16 = jnp.bfloat16
F32 = jnp.float32


def span(step, size, low, high):
    if step == 0:
        return 0, low, size
    if step == 1:
        return size - low, 0, low
    return 0, low + size, high


def exchange(tms, rows, low, high, x_ref, p_ref, send_sem, recv_sem):
    tm, row = lax.axis_index("tm"), lax.axis_index("row")
    frames, height = x_ref.shape[:2]

    def there(dt, dr):
        t, r = tm + dt, row + dr
        return (t >= 0) & (t < tms) & (r >= 0) & (r < rows)

    barrier = pltpu.get_barrier_semaphore()
    for dt, dr in SIDES:

        @pl.when(there(dt, dr))
        def _():
            pl.semaphore_signal(
                barrier, inc=1, device_id=(tm + dt, row + dr), device_id_type=MESH
            )

    peers = sum(there(dt, dr).astype(jnp.int32) for dt, dr in SIDES)
    pl.semaphore_wait(barrier, peers)

    def copy(k):
        dt, dr = SIDES[k]
        t_from, t_to, t_len = span(dt, frames, 1, 1)
        r_from, r_to, r_len = span(dr, height, low, high)
        return pltpu.make_async_remote_copy(
            src_ref=x_ref.at[pl.ds(t_from, t_len), pl.ds(r_from, r_len)],
            dst_ref=p_ref.at[pl.ds(t_to, t_len), pl.ds(r_to, r_len)],
            send_sem=send_sem.at[k],
            recv_sem=recv_sem.at[k],
            device_id=(tm + dt, row + dr),
            device_id_type=MESH,
        )

    for k, (dt, dr) in enumerate(SIDES):

        @pl.when(there(dt, dr))
        def _():
            copy(k).start()

    for k, (dt, dr) in enumerate(SIDES):
        _, t_to, t_len = span(dt, frames, 1, 1)
        _, r_to, r_len = span(dr, height, low, high)

        @pl.when(jnp.logical_not(there(-dt, -dr)))
        def _():
            def clear(t, carry):
                p_ref[t_to + t, r_to : r_to + r_len] = jnp.zeros(
                    (r_len,) + p_ref.shape[2:], p_ref.dtype
                )
                return carry

            lax.fori_loop(0, t_len, clear, 0)

    def arrive():
        for k, (dt, dr) in enumerate(SIDES):

            @pl.when(there(-dt, -dr))
            def _():
                copy(k).wait_recv()

            @pl.when(there(dt, dr))
            def _():
                copy(k).wait_send()

    return arrive


def halo_kernel(tms, rows, low, high, x_ref, p_ref, own_sem, send_sem, recv_sem):
    frames, height = x_ref.shape[:2]
    own = pltpu.make_async_copy(
        x_ref, p_ref.at[pl.ds(1, frames), pl.ds(low, height)], own_sem
    )
    own.start()
    exchange(tms, rows, low, high, x_ref, p_ref, send_sem, recv_sem)()
    own.wait()


def halo(x, mesh, low, high, collective_id):
    frames, height = x.shape[:2]
    return pl.pallas_call(
        functools.partial(halo_kernel, mesh.shape["tm"], mesh.shape["row"], low, high),
        out_shape=jax.ShapeDtypeStruct((frames + 2, height + low + high) + x.shape[2:], x.dtype),
        in_specs=[pl.BlockSpec(memory_space=pltpu.VMEM)],
        out_specs=pl.BlockSpec(memory_space=pltpu.VMEM),
        scratch_shapes=[
            pltpu.SemaphoreType.DMA,
            pltpu.SemaphoreType.DMA((len(SIDES),)),
            pltpu.SemaphoreType.DMA((len(SIDES),)),
        ],
        compiler_params=pltpu.CompilerParams(
            collective_id=collective_id, has_side_effects=True, vmem_limit_bytes=32 << 20
        ),
        name="halo",
    )(x)


def nt(a, b):
    return lax.dot_general(a, b, (((1,), (1,)), ((), ())), preferred_element_type=F32)


def dot(a, b):
    return jnp.dot(a, b, preferred_element_type=F32)


def one_hot(rows, columns, at):
    row = lax.broadcasted_iota(jnp.int32, (rows, columns), 0)
    column = lax.broadcasted_iota(jnp.int32, (rows, columns), 1)
    return jnp.where(column == at(row), 1.0, 0.0).astype(BF16)


def shifted(x, axis):
    size = x.shape[axis]
    wide = x.astype(F32)
    place = lax.broadcasted_iota(jnp.int32, x.shape, axis)
    before = jnp.where(place == 0, 0.0, pltpu.roll(wide, 1, axis)).astype(BF16)
    after = jnp.where(place == size - 1, 0.0, pltpu.roll(wide, size - 1, axis)).astype(BF16)
    return before, after


def first_kernel(
    tms, rows, x_ref, w1_ref, t1_ref, d_ref, out_ref,
    p_s, even_s, odd_s, lower_s, upper_s, d_s, c_s, z_s, s_s, g_s, send_sem, recv_sem,
):
    arrive = exchange(tms, rows, 2, 1, x_ref, p_s, send_sem, recv_sem)
    first_compute(
        arrive, x_ref, w1_ref, t1_ref, d_ref, out_ref,
        p_s, even_s, odd_s, lower_s, upper_s, d_s, c_s, z_s, s_s, g_s,
    )


def first_compute(
    arrive, x_ref, w1_ref, t1_ref, d_ref, out_ref,
    p_s, even_s, odd_s, lower_s, upper_s, d_s, c_s, z_s, s_s, g_s,
):
    frames, height, c1, width = x_ref.shape
    m1, c2 = w1_ref.shape[3], d_ref.shape[3]
    half = width // 2
    kept = height + 1

    for b in range(3):
        odd_s[b, :c1, :] = jnp.zeros((c1, m1), BF16)
        d_s[b, :c1, :] = jnp.zeros((c1, c2), BF16)
        for a in range(3):
            even_s[b, a * c1 : (a + 1) * c1, :] = w1_ref[a, b]
            odd_s[b, (a + 1) * c1 : (a + 2) * c1, :] = w1_ref[a, b]
            d_s[b, (a + 1) * c1 : (a + 2) * c1, :] = d_ref[a, b]
    nothing = jnp.zeros((c1, m1), BF16)
    taps = [t1_ref[k] for k in range(3)]
    lower_s[...] = jnp.concatenate([taps[0], taps[1], taps[2], nothing], axis=0).T
    upper_s[...] = jnp.concatenate([taps[1], taps[0], nothing, taps[2]], axis=0).T

    move = one_hot(3 * width, width, lambda row: lax.rem(row, width) + row // width - 1)
    pick = one_hot(3 * half, width, lambda row: 2 * lax.rem(row, half) + row // half - 1)

    def at(t, count):
        return pl.ds(pl.multiple_of(t * width, width), count * width)

    def columns(x, t, start):
        x = x.reshape(x.shape[0] * c1, width)
        moved = nt(move, x).astype(BF16)
        for b in range(3):
            c_s[b, at(t, 1), start : start + x.shape[0]] = moved[b * width : (b + 1) * width]

    def middles(t, count, hs):
        for h in hs:
            start = c1 * (h - h % 2)
            total = None
            for b in range(3):
                if h % 2 == 0:
                    part = dot(c_s[b, at(t, count), start : start + 3 * c1], even_s[b])
                else:
                    part = dot(c_s[b, at(t, count), start : start + 4 * c1], odd_s[b])
                total = part if total is None else total + part
            middle = jnp.maximum(total, 0.0).astype(BF16)
            z_s[h, at(t, count), :] = dot(middle, (upper_s if h % 2 == 0 else lower_s)[...])

    def inner(q, carry):
        for f in range(2):
            columns(x_ref[2 * q + f], 2 * q + f + 1, 2 * c1)
        middles(2 * q + 1, 2, range(2, height))
        return carry

    lax.fori_loop(0, frames // 2, inner, 0)
    arrive()

    def edges(q, carry):
        for f in range(2):
            t = 2 * q + f + 1
            columns(p_s[t, 0:2], t, 0)
            columns(p_s[t, height + 2 : height + 3], t, c1 * (height + 2))
        middles(2 * q + 1, 2, (0, 1, height))
        return carry

    lax.fori_loop(0, frames // 2, edges, 0)

    def outer(q, carry):
        t = q * (frames + 1)
        columns(p_s[t], t, 0)
        middles(t, 1, range(kept))
        return carry

    lax.fori_loop(0, 2, outer, 0)

    top = jnp.where(lax.axis_index("row") == 0, 0.0, 1.0)
    first_half = lax.broadcasted_iota(jnp.int32, (width, 2 * c1), 1) < c1

    def section(f, carry):
        for p in range(height // 2 + 1):
            lo, up = 2 * p - 1, 2 * p
            s = c_s[1, at(f + 1, 1), 2 * c1 * p : 2 * c1 * (p + 1)].astype(F32)
            lanes, last = slice(0, 2 * c1), slice(2 * c1, 4 * c1)
            if p == 0:
                s = s + z_s[up, at(f, 1), lanes]
                s = s + pltpu.roll(z_s[up, at(f + 1, 1), lanes], c1, 1)
                s = s + z_s[up, at(f + 2, 1), last]
                s = jnp.where(first_half, 0.0, jnp.maximum(s, 0.0) * top)
            else:
                s = s + jnp.where(first_half, z_s[lo, at(f, 1), lanes], z_s[up, at(f, 1), lanes])
                swapped = jnp.where(
                    first_half, z_s[up, at(f + 1, 1), lanes], z_s[lo, at(f + 1, 1), lanes]
                )
                s = s + pltpu.roll(swapped, c1, 1)
                s = s + z_s[lo, at(f + 2, 1), last] + z_s[up, at(f + 2, 1), last]
                s = jnp.maximum(s, 0.0)
            s_s[:, lanes.stop * p : lanes.stop * (p + 1)] = s.astype(BF16)
        g = dot(pick, s_s[...]).astype(BF16)
        where = pl.ds(pl.multiple_of(f * half, half), half)
        for b in range(3):
            g_s[b, where, :] = g[b * half : (b + 1) * half]
        return carry

    lax.fori_loop(0, frames, section, 0)

    group = 4

    def down(q, carry):
        where = pl.ds(pl.multiple_of(q * group * half, group * half), group * half)
        for i in range(height // 2):
            total = None
            for b in range(3):
                part = dot(g_s[b, where, 2 * c1 * i : 2 * c1 * i + 4 * c1], d_s[b])
                total = part if total is None else total + part
            total = jnp.maximum(total, 0.0).astype(BF16)
            out_ref[pl.ds(q * group, group), i] = total.reshape(group, half, c2)
        return carry

    lax.fori_loop(0, frames // group, down, 0)


def first(x, mesh, spatial_one, temporal_one, down_weight):
    frames, height, c1, width = x.shape
    m1, c2 = spatial_one.shape[3], down_weight.shape[3]
    kept = height + 1
    vmem = pl.BlockSpec(memory_space=pltpu.VMEM)
    pixels = (frames + 2) * width
    return pl.pallas_call(
        functools.partial(first_kernel, mesh.shape["tm"], mesh.shape["row"]),
        out_shape=jax.ShapeDtypeStruct((frames, height // 2, width // 2, c2), BF16),
        in_specs=[vmem] * 4,
        out_specs=vmem,
        scratch_shapes=[
            pltpu.VMEM((frames + 2, height + 3, c1, width), BF16),
            pltpu.VMEM((3, 3 * c1, m1), BF16),
            pltpu.VMEM((3, 4 * c1, m1), BF16),
            pltpu.VMEM((m1, 4 * c1), BF16),
            pltpu.VMEM((m1, 4 * c1), BF16),
            pltpu.VMEM((3, 4 * c1, c2), BF16),
            pltpu.VMEM((3, pixels, (height + 3) * c1), BF16),
            pltpu.VMEM((kept, pixels, 4 * c1), F32),
            pltpu.VMEM((width, (kept + 1) * c1), BF16),
            pltpu.VMEM((3, frames * width // 2, (kept + 1) * c1), BF16),
            pltpu.SemaphoreType.DMA((len(SIDES),)),
            pltpu.SemaphoreType.DMA((len(SIDES),)),
        ],
        compiler_params=pltpu.CompilerParams(
            collective_id=0, has_side_effects=True, vmem_limit_bytes=52 << 20
        ),
        name="first",
    )(x, spatial_one, temporal_one, down_weight)


def second_kernel(p_ref, w2_ref, t2_ref, out_ref, w_s, v_s, m_s):
    frames, height = out_ref.shape[:2]
    width, c2 = p_ref.shape[2:]
    for a in range(3):
        for b in range(3):
            k = (3 * a + b) * c2
            w_s[k : k + c2, :] = w2_ref[a, b].T

    def columns(t, carry):
        rows = pl.ds(pl.multiple_of(t * width, width), width)
        for i in range(height + 2):
            x = p_ref[t, i]
            before, after = shifted(x, 0)
            v_s[i, rows, :c2] = before
            v_s[i, rows, c2 : 2 * c2] = x
            v_s[i, rows, 2 * c2 :] = after
        return carry

    lax.fori_loop(0, frames + 2, columns, 0)

    group = 3

    def spatial(q, carry):
        rows = pl.ds(pl.multiple_of(q * group * width, group * width), group * width)
        for i in range(height):
            lhs = jnp.concatenate([v_s[i + a, rows, :] for a in range(3)], axis=1)
            middle = jnp.dot(lhs, w_s[...], preferred_element_type=F32)
            m_s[i, rows, :] = jnp.maximum(middle, 0.0).astype(BF16)
        return carry

    lax.fori_loop(0, (frames + 2) // group, spatial, 0)

    span_t = 4

    def temporal(q, carry):
        for i in range(height):
            total = p_ref[pl.ds(q * span_t + 1, span_t), i + 1].astype(F32)
            total = total.reshape(span_t * width, c2)
            for k in range(3):
                start = pl.multiple_of((q * span_t + k) * width, width)
                lhs = m_s[i, pl.ds(start, span_t * width), :]
                total = total + jnp.dot(lhs, t2_ref[k], preferred_element_type=F32)
            total = jnp.maximum(total, 0.0).astype(BF16)
            out_ref[pl.ds(q * span_t, span_t), i] = total.reshape(span_t, width, c2)
        return carry

    lax.fori_loop(0, frames // span_t, temporal, 0)


def second(padded, spatial_two, temporal_two):
    frames, height = padded.shape[0] - 2, padded.shape[1] - 2
    width, c2 = padded.shape[2:]
    m2 = spatial_two.shape[2]
    vmem = pl.BlockSpec(memory_space=pltpu.VMEM)
    return pl.pallas_call(
        second_kernel,
        out_shape=jax.ShapeDtypeStruct((frames, height, width, c2), BF16),
        in_specs=[vmem] * 3,
        out_specs=vmem,
        scratch_shapes=[
            pltpu.VMEM((9 * c2, m2), BF16),
            pltpu.VMEM((height + 2, (frames + 2) * width, 3 * c2), BF16),
            pltpu.VMEM((height, (frames + 2) * width, m2), BF16),
        ],
        compiler_params=pltpu.CompilerParams(vmem_limit_bytes=48 << 20),
        name="second",
    )(padded, spatial_two, temporal_two)


def on_device(mesh, video_clip, spatial_one, temporal_one, down_weight, spatial_two, temporal_two):
    down = jnp.transpose(down_weight, (0, 1, 3, 2))
    one = jnp.transpose(spatial_one, (0, 1, 3, 2))
    temporal = jnp.transpose(temporal_two, (0, 2, 1))
    reduced = first(video_clip, mesh, one, temporal_one, down)
    padded = halo(reduced, mesh, 1, 1, 1)
    return second(padded, spatial_two, temporal)


def solution(mesh):
    placed = (P("tm", "row", None, None), P(), P(), P(), P(), P())
    return jax.shard_map(
        functools.partial(on_device, mesh),
        mesh=mesh,
        in_specs=placed,
        out_specs=P("tm", "row", None, None),
        check_vma=False,
    )
```

```python
import functools

import jax
import jax.numpy as jnp
from jax import lax
from jax.experimental import pallas as pl
from jax.experimental.pallas import tpu as pltpu
from jax.sharding import PartitionSpec as P

MESH = pl.DeviceIdType.MESH
SIDES = [(dt, dr) for dt in (-1, 0, 1) for dr in (-1, 0, 1) if (dt, dr) != (0, 0)]
BF16 = jnp.bfloat16
F32 = jnp.float32


def span(step, size, low, high):
    if step == 0:
        return 0, low, size
    if step == 1:
        return size - low, 0, low
    return 0, low + size, high


def exchange(tms, rows, low, high, x_ref, p_ref, send_sem, recv_sem):
    tm, row = lax.axis_index("tm"), lax.axis_index("row")
    frames, height = x_ref.shape[:2]

    def there(dt, dr):
        t, r = tm + dt, row + dr
        return (t >= 0) & (t < tms) & (r >= 0) & (r < rows)

    barrier = pltpu.get_barrier_semaphore()
    for dt, dr in SIDES:

        @pl.when(there(dt, dr))
        def _():
            pl.semaphore_signal(
                barrier, inc=1, device_id=(tm + dt, row + dr), device_id_type=MESH
            )

    peers = sum(there(dt, dr).astype(jnp.int32) for dt, dr in SIDES)
    pl.semaphore_wait(barrier, peers)

    def copy(k):
        dt, dr = SIDES[k]
        t_from, t_to, t_len = span(dt, frames, 1, 1)
        r_from, r_to, r_len = span(dr, height, low, high)
        return pltpu.make_async_remote_copy(
            src_ref=x_ref.at[pl.ds(t_from, t_len), pl.ds(r_from, r_len)],
            dst_ref=p_ref.at[pl.ds(t_to, t_len), pl.ds(r_to, r_len)],
            send_sem=send_sem.at[k],
            recv_sem=recv_sem.at[k],
            device_id=(tm + dt, row + dr),
            device_id_type=MESH,
        )

    for k, (dt, dr) in enumerate(SIDES):

        @pl.when(there(dt, dr))
        def _():
            copy(k).start()

    for k, (dt, dr) in enumerate(SIDES):
        _, t_to, t_len = span(dt, frames, 1, 1)
        _, r_to, r_len = span(dr, height, low, high)

        @pl.when(jnp.logical_not(there(-dt, -dr)))
        def _():
            def clear(t, carry):
                p_ref[t_to + t, r_to : r_to + r_len] = jnp.zeros(
                    (r_len,) + p_ref.shape[2:], p_ref.dtype
                )
                return carry

            lax.fori_loop(0, t_len, clear, 0)

    def arrive():
        for k, (dt, dr) in enumerate(SIDES):

            @pl.when(there(-dt, -dr))
            def _():
                copy(k).wait_recv()

            @pl.when(there(dt, dr))
            def _():
                copy(k).wait_send()

    return arrive


def nt(a, b):
    return lax.dot_general(a, b, (((1,), (1,)), ((), ())), preferred_element_type=F32)


def shifted(x, axis):
    size = x.shape[axis]
    wide = x.astype(F32)
    place = lax.broadcasted_iota(jnp.int32, x.shape, axis)
    before = jnp.where(place == 0, 0.0, pltpu.roll(wide, 1, axis)).astype(BF16)
    after = jnp.where(place == size - 1, 0.0, pltpu.roll(wide, size - 1, axis)).astype(BF16)
    return before, after


def first_kernel(
    tms, rows, x_ref, w1_ref, t1_ref, d_ref, out_ref,
    p_s, w_s, col_s, z_s, s_s, g_s, send_sem, recv_sem,
):
    arrive = exchange(tms, rows, 2, 1, x_ref, p_s, send_sem, recv_sem)
    frames, height, c1, width = x_ref.shape
    m1 = w1_ref.shape[3]
    half = width // 2
    kept = height + 1
    for a in range(3):
        for b in range(3):
            k = (3 * a + b) * c1
            w_s[:, k : k + c1] = w1_ref[a, b].T
    taps = t1_ref[...].reshape(3 * c1, m1)

    def columns(slot, f, r, x):
        before, after = shifted(x, 1)
        lanes = slice(f * width, (f + 1) * width)
        k = 3 * c1 * r
        col_s[slot, k : k + c1, lanes] = before
        col_s[slot, k + c1 : k + 2 * c1, lanes] = x
        col_s[slot, k + 2 * c1 : k + 3 * c1, lanes] = after

    def middles(slot, t_one, t_two, hs):
        for h in hs:
            col = col_s[slot, 3 * c1 * h : 3 * c1 * (h + 3), :]
            middle = jnp.dot(w_s[...], col, preferred_element_type=F32)
            middle = jnp.maximum(middle, 0.0).astype(BF16)
            z = jnp.dot(taps, middle, preferred_element_type=F32)
            z_s[t_one, h] = z[:, :width]
            z_s[t_two, h] = z[:, width:]

    def inner(q, carry):
        for r in range(2, height + 2):
            for f in range(2):
                columns(q, f, r, x_ref[2 * q + f, r - 2])
        middles(q, 2 * q + 1, 2 * q + 2, range(2, height))
        return carry

    lax.fori_loop(0, frames // 2, inner, 0)
    arrive()

    def edges(q, carry):
        for r in (0, 1, height + 2):
            for f in range(2):
                columns(q, f, r, p_s[2 * q + f + 1, r])
        middles(q, 2 * q + 1, 2 * q + 2, (0, 1, height))
        return carry

    lax.fori_loop(0, frames // 2, edges, 0)

    slot, ends = frames // 2, (0, frames + 1)
    for r in range(height + 3):
        for f in range(2):
            columns(slot, f, r, p_s[ends[f], r])
    middles(slot, *ends, range(kept))

    top = jnp.where(lax.axis_index("row") == 0, 0.0, 1.0)
    tap = lax.broadcasted_iota(jnp.int32, (3 * half, width), 0)
    column = lax.broadcasted_iota(jnp.int32, (3 * half, width), 1)
    pick = column == 2 * lax.rem(tap, half) + tap // half - 1
    pick = jnp.where(pick, 1.0, 0.0).astype(BF16)

    def section(f, carry):
        for h in range(kept):
            source = p_s[f + 1, 1] if h == 0 else x_ref[f, h - 1]
            s = source.astype(F32) + z_s[f, h, :c1]
            s = s + z_s[f + 1, h, c1 : 2 * c1] + z_s[f + 2, h, 2 * c1 :]
            s = jnp.maximum(s, 0.0)
            if h == 0:
                s = s * top
            s_s[h * c1 : (h + 1) * c1, :] = s.astype(BF16)
        g = nt(pick, s_s[...]).astype(BF16)
        rows = pl.ds(pl.multiple_of(f * half, half), half)
        for b in range(3):
            g_s[b, rows, :] = g[b * half : (b + 1) * half]
        return carry

    lax.fori_loop(0, frames, section, 0)

    group = 4

    def down(q, carry):
        rows = pl.ds(pl.multiple_of(q * group * half, group * half), group * half)
        for i in range(height // 2):
            total = None
            for b in range(3):
                lhs = g_s[b, rows, 2 * c1 * i : 2 * c1 * i + 3 * c1]
                rhs = jnp.concatenate([d_ref[a, b] for a in range(3)], axis=0)
                part = jnp.dot(lhs, rhs, preferred_element_type=F32)
                total = part if total is None else total + part
            total = jnp.maximum(total, 0.0).astype(BF16)
            out_ref[pl.ds(q * group, group), i] = total.reshape(group, half, total.shape[1])
        return carry

    lax.fori_loop(0, frames // group, down, 0)


def first(x, mesh, spatial_one, temporal_one, down_weight):
    frames, height, c1, width = x.shape
    m1, c2 = spatial_one.shape[3], down_weight.shape[3]
    kept = height + 1
    vmem = pl.BlockSpec(memory_space=pltpu.VMEM)
    return pl.pallas_call(
        functools.partial(first_kernel, mesh.shape["tm"], mesh.shape["row"]),
        out_shape=jax.ShapeDtypeStruct((frames, height // 2, width // 2, c2), BF16),
        in_specs=[vmem] * 4,
        out_specs=vmem,
        scratch_shapes=[
            pltpu.VMEM((frames + 2, height + 3, c1, width), BF16),
            pltpu.VMEM((m1, 9 * c1), BF16),
            pltpu.VMEM((frames // 2 + 1, 3 * c1 * (height + 3), 2 * width), BF16),
            pltpu.VMEM((frames + 2, kept, 3 * c1, width), F32),
            pltpu.VMEM((kept * c1, width), BF16),
            pltpu.VMEM((3, frames * width // 2, kept * c1), BF16),
            pltpu.SemaphoreType.DMA((len(SIDES),)),
            pltpu.SemaphoreType.DMA((len(SIDES),)),
        ],
        compiler_params=pltpu.CompilerParams(
            collective_id=0, has_side_effects=True, vmem_limit_bytes=50 << 20
        ),
        name="first",
    )(x, spatial_one, temporal_one, down_weight)


def second_kernel(
    tms, devices, x_ref, w2_ref, t2_ref, out_ref, p_s, w_s, v_s, m_s, send_sem, recv_sem
):
    arrive = exchange(tms, devices, 1, 1, x_ref, p_s, send_sem, recv_sem)
    frames, height, width, c2 = x_ref.shape
    for a in range(3):
        for b in range(3):
            k = (3 * a + b) * c2
            w_s[k : k + c2, :] = w2_ref[a, b].T

    def at(t, count):
        return pl.ds(pl.multiple_of(t * width, width), count * width)

    def columns(t, i, x):
        before, after = shifted(x, 0)
        v_s[i, at(t, 1), :c2] = before
        v_s[i, at(t, 1), c2 : 2 * c2] = x
        v_s[i, at(t, 1), 2 * c2 :] = after

    def window(i, t, count):
        return jnp.concatenate([v_s[i + a, at(t, count), :] for a in range(3)], axis=1)

    def middle(lhs):
        total = jnp.dot(lhs, w_s[...], preferred_element_type=F32)
        return jnp.maximum(total, 0.0).astype(BF16)

    group = 4

    def inner(q, carry):
        t = q * group + 1
        for f in range(group):
            for i in range(height):
                columns(t + f, i + 1, x_ref[q * group + f, i])
        for i in range(1, height - 1):
            m_s[i, at(t, group), :] = middle(window(i, t, group))
        return carry

    lax.fori_loop(0, frames // group, inner, 0)
    arrive()

    def edges(q, carry):
        t = q * group + 1
        for f in range(group):
            for i in (0, height + 1):
                columns(t + f, i, p_s[t + f, i])
        for i in (0, height - 1):
            m_s[i, at(t, group), :] = middle(window(i, t, group))
        return carry

    lax.fori_loop(0, frames // group, edges, 0)

    def outer(q, carry):
        t = q * (frames + 1)
        for i in range(height + 2):
            columns(t, i, p_s[t, i])
        found = middle(jnp.concatenate([window(i, t, 1) for i in range(height)], axis=0))
        for i in range(height):
            m_s[i, at(t, 1), :] = found[i * width : (i + 1) * width]
        return carry

    lax.fori_loop(0, 2, outer, 0)

    def temporal(q, carry):
        for i in range(height):
            total = x_ref[pl.ds(q * group, group), i].astype(F32).reshape(group * width, c2)
            for k in range(3):
                lhs = m_s[i, at(q * group + k, group), :]
                total = total + jnp.dot(lhs, t2_ref[k], preferred_element_type=F32)
            total = jnp.maximum(total, 0.0).astype(BF16)
            out_ref[pl.ds(q * group, group), i] = total.reshape(group, width, c2)
        return carry

    lax.fori_loop(0, frames // group, temporal, 0)


def second(x, mesh, spatial_two, temporal_two):
    frames, height, width, c2 = x.shape
    m2 = spatial_two.shape[2]
    vmem = pl.BlockSpec(memory_space=pltpu.VMEM)
    return pl.pallas_call(
        functools.partial(second_kernel, mesh.shape["tm"], mesh.shape["row"]),
        out_shape=jax.ShapeDtypeStruct((frames, height, width, c2), BF16),
        in_specs=[vmem] * 3,
        out_specs=vmem,
        scratch_shapes=[
            pltpu.VMEM((frames + 2, height + 2, width, c2), BF16),
            pltpu.VMEM((9 * c2, m2), BF16),
            pltpu.VMEM((height + 2, (frames + 2) * width, 3 * c2), BF16),
            pltpu.VMEM((height, (frames + 2) * width, m2), BF16),
            pltpu.SemaphoreType.DMA((len(SIDES),)),
            pltpu.SemaphoreType.DMA((len(SIDES),)),
        ],
        compiler_params=pltpu.CompilerParams(
            collective_id=1, has_side_effects=True, vmem_limit_bytes=48 << 20
        ),
        name="second",
    )(x, spatial_two, temporal_two)


def on_device(mesh, video_clip, spatial_one, temporal_one, down_weight, spatial_two, temporal_two):
    down = jnp.transpose(down_weight, (0, 1, 3, 2))
    one = jnp.transpose(spatial_one, (0, 1, 3, 2))
    temporal = jnp.transpose(temporal_two, (0, 2, 1))
    reduced = first(video_clip, mesh, one, temporal_one, down)
    return second(reduced, mesh, spatial_two, temporal)


def solution(mesh):
    placed = (P("tm", "row", None, None), P(), P(), P(), P(), P())
    return jax.shard_map(
        functools.partial(on_device, mesh),
        mesh=mesh,
        in_specs=placed,
        out_specs=P("tm", "row", None, None),
        check_vma=False,
    )
```

```python
import functools

import jax
import jax.numpy as jnp
from jax import lax
from jax.experimental import pallas as pl
from jax.experimental.pallas import tpu as pltpu
from jax.sharding import PartitionSpec as P

MESH = pl.DeviceIdType.MESH
SIDES = [(dt, dr) for dt in (-1, 0, 1) for dr in (-1, 0, 1) if (dt, dr) != (0, 0)]
BF16 = jnp.bfloat16
F32 = jnp.float32


def span(step, size, low, high):
    if step == 0:
        return 0, low, size
    if step == 1:
        return size - low, 0, low
    return 0, low + size, high


def exchange(tms, rows, low, high, x_ref, p_ref, send_sem, recv_sem):
    tm, row = lax.axis_index("tm"), lax.axis_index("row")
    frames, height = x_ref.shape[:2]

    def there(dt, dr):
        t, r = tm + dt, row + dr
        return (t >= 0) & (t < tms) & (r >= 0) & (r < rows)

    barrier = pltpu.get_barrier_semaphore()
    for dt, dr in SIDES:

        @pl.when(there(dt, dr))
        def _():
            pl.semaphore_signal(
                barrier, inc=1, device_id=(tm + dt, row + dr), device_id_type=MESH
            )

    peers = sum(there(dt, dr).astype(jnp.int32) for dt, dr in SIDES)
    pl.semaphore_wait(barrier, peers)

    def copy(k):
        dt, dr = SIDES[k]
        t_from, t_to, t_len = span(dt, frames, 1, 1)
        r_from, r_to, r_len = span(dr, height, low, high)
        return pltpu.make_async_remote_copy(
            src_ref=x_ref.at[pl.ds(t_from, t_len), pl.ds(r_from, r_len)],
            dst_ref=p_ref.at[pl.ds(t_to, t_len), pl.ds(r_to, r_len)],
            send_sem=send_sem.at[k],
            recv_sem=recv_sem.at[k],
            device_id=(tm + dt, row + dr),
            device_id_type=MESH,
        )

    for k, (dt, dr) in enumerate(SIDES):

        @pl.when(there(dt, dr))
        def _():
            copy(k).start()

    for k, (dt, dr) in enumerate(SIDES):
        _, t_to, t_len = span(dt, frames, 1, 1)
        _, r_to, r_len = span(dr, height, low, high)

        @pl.when(jnp.logical_not(there(-dt, -dr)))
        def _():
            def clear(t, carry):
                p_ref[t_to + t, r_to : r_to + r_len] = jnp.zeros(
                    (r_len,) + p_ref.shape[2:], p_ref.dtype
                )
                return carry

            lax.fori_loop(0, t_len, clear, 0)

    def arrive():
        for k, (dt, dr) in enumerate(SIDES):

            @pl.when(there(-dt, -dr))
            def _():
                copy(k).wait_recv()

            @pl.when(there(dt, dr))
            def _():
                copy(k).wait_send()

    return arrive


def nt(a, b):
    return lax.dot_general(a, b, (((1,), (1,)), ((), ())), preferred_element_type=F32)


def shifted(x, axis):
    size = x.shape[axis]
    wide = x.astype(F32)
    place = lax.broadcasted_iota(jnp.int32, x.shape, axis)
    before = jnp.where(place == 0, 0.0, pltpu.roll(wide, 1, axis)).astype(BF16)
    after = jnp.where(place == size - 1, 0.0, pltpu.roll(wide, size - 1, axis)).astype(BF16)
    return before, after


def first_kernel(
    tms, rows, x_hbm, w1_hbm, t1_hbm, d_hbm, out_ref,
    x_ref, w1_ref, t1_ref, d_ref, p_s, w_s, col_s, z_s, s_s, g_s, load_sem, send_sem, recv_sem,
):
    pairs = ((x_hbm, x_ref), (w1_hbm, w1_ref), (t1_hbm, t1_ref), (d_hbm, d_ref))
    loads = [
        pltpu.make_async_copy(source, target, load_sem.at[n])
        for n, (source, target) in enumerate(pairs)
    ]
    for load in loads:
        load.start()
    arrive = exchange(tms, rows, 2, 1, x_hbm, p_s, send_sem, recv_sem)
    for load in loads:
        load.wait()
    frames, height, c1, width = x_ref.shape
    m1 = w1_ref.shape[3]
    half = width // 2
    kept = height + 1
    for a in range(3):
        for b in range(3):
            k = (3 * a + b) * c1
            w_s[:, k : k + c1] = w1_ref[a, b].T
    taps = t1_ref[...].reshape(3 * c1, m1)

    def columns(slot, f, r, x):
        before, after = shifted(x, 1)
        lanes = slice(f * width, (f + 1) * width)
        k = 3 * c1 * r
        col_s[slot, k : k + c1, lanes] = before
        col_s[slot, k + c1 : k + 2 * c1, lanes] = x
        col_s[slot, k + 2 * c1 : k + 3 * c1, lanes] = after

    def middles(slot, t_one, t_two, hs):
        for h in hs:
            col = col_s[slot, 3 * c1 * h : 3 * c1 * (h + 3), :]
            middle = jnp.dot(w_s[...], col, preferred_element_type=F32)
            middle = jnp.maximum(middle, 0.0).astype(BF16)
            z = jnp.dot(taps, middle, preferred_element_type=F32)
            z_s[t_one, h] = z[:, :width]
            z_s[t_two, h] = z[:, width:]

    def inner(q, carry):
        for r in range(2, height + 2):
            for f in range(2):
                columns(q, f, r, x_ref[2 * q + f, r - 2])
        middles(q, 2 * q + 1, 2 * q + 2, range(2, height))
        return carry

    lax.fori_loop(0, frames // 2, inner, 0)
    arrive()

    def edges(q, carry):
        for r in (0, 1, height + 2):
            for f in range(2):
                columns(q, f, r, p_s[2 * q + f + 1, r])
        middles(q, 2 * q + 1, 2 * q + 2, (0, 1, height))
        return carry

    lax.fori_loop(0, frames // 2, edges, 0)

    slot, ends = frames // 2, (0, frames + 1)
    for r in range(height + 3):
        for f in range(2):
            columns(slot, f, r, p_s[ends[f], r])
    middles(slot, *ends, range(kept))

    top = jnp.where(lax.axis_index("row") == 0, 0.0, 1.0)
    tap = lax.broadcasted_iota(jnp.int32, (3 * half, width), 0)
    column = lax.broadcasted_iota(jnp.int32, (3 * half, width), 1)
    pick = column == 2 * lax.rem(tap, half) + tap // half - 1
    pick = jnp.where(pick, 1.0, 0.0).astype(BF16)

    def section(f, carry):
        for h in range(kept):
            source = p_s[f + 1, 1] if h == 0 else x_ref[f, h - 1]
            s = source.astype(F32) + z_s[f, h, :c1]
            s = s + z_s[f + 1, h, c1 : 2 * c1] + z_s[f + 2, h, 2 * c1 :]
            s = jnp.maximum(s, 0.0)
            if h == 0:
                s = s * top
            s_s[h * c1 : (h + 1) * c1, :] = s.astype(BF16)
        g = nt(pick, s_s[...]).astype(BF16)
        rows = pl.ds(pl.multiple_of(f * half, half), half)
        for b in range(3):
            g_s[b, rows, :] = g[b * half : (b + 1) * half]
        return carry

    lax.fori_loop(0, frames, section, 0)

    group = 4

    def down(q, carry):
        rows = pl.ds(pl.multiple_of(q * group * half, group * half), group * half)
        for i in range(height // 2):
            total = None
            for b in range(3):
                lhs = g_s[b, rows, 2 * c1 * i : 2 * c1 * i + 3 * c1]
                rhs = jnp.concatenate([d_ref[a, b] for a in range(3)], axis=0)
                part = jnp.dot(lhs, rhs, preferred_element_type=F32)
                total = part if total is None else total + part
            total = jnp.maximum(total, 0.0).astype(BF16)
            out_ref[pl.ds(q * group, group), i] = total.reshape(group, half, total.shape[1])
        return carry

    lax.fori_loop(0, frames // group, down, 0)


def first(x, mesh, spatial_one, temporal_one, down_weight):
    frames, height, c1, width = x.shape
    m1, c2 = spatial_one.shape[3], down_weight.shape[3]
    kept = height + 1
    vmem = pl.BlockSpec(memory_space=pltpu.VMEM)
    return pl.pallas_call(
        functools.partial(first_kernel, mesh.shape["tm"], mesh.shape["row"]),
        out_shape=jax.ShapeDtypeStruct((frames, height // 2, width // 2, c2), BF16),
        in_specs=[pl.BlockSpec(memory_space=pltpu.HBM)] * 4,
        out_specs=vmem,
        scratch_shapes=[
            pltpu.VMEM(x.shape, BF16),
            pltpu.VMEM(spatial_one.shape, BF16),
            pltpu.VMEM(temporal_one.shape, BF16),
            pltpu.VMEM(down_weight.shape, BF16),
            pltpu.VMEM((frames + 2, height + 3, c1, width), BF16),
            pltpu.VMEM((m1, 9 * c1), BF16),
            pltpu.VMEM((frames // 2 + 1, 3 * c1 * (height + 3), 2 * width), BF16),
            pltpu.VMEM((frames + 2, kept, 3 * c1, width), F32),
            pltpu.VMEM((kept * c1, width), BF16),
            pltpu.VMEM((3, frames * width // 2, kept * c1), BF16),
            pltpu.SemaphoreType.DMA((4,)),
            pltpu.SemaphoreType.DMA((len(SIDES),)),
            pltpu.SemaphoreType.DMA((len(SIDES),)),
        ],
        compiler_params=pltpu.CompilerParams(
            collective_id=0, has_side_effects=True, vmem_limit_bytes=63 << 20
        ),
        name="first",
    )(x, spatial_one, temporal_one, down_weight)


def second_kernel(
    tms, devices, x_ref, w2_ref, t2_ref, out_ref, p_s, w_s, v_s, m_s, send_sem, recv_sem
):
    arrive = exchange(tms, devices, 1, 1, x_ref, p_s, send_sem, recv_sem)
    frames, height, width, c2 = x_ref.shape
    for a in range(3):
        for b in range(3):
            k = (3 * a + b) * c2
            w_s[k : k + c2, :] = w2_ref[a, b].T

    def at(t, count):
        return pl.ds(pl.multiple_of(t * width, width), count * width)

    def columns(t, i, x):
        before, after = shifted(x, 0)
        v_s[i, at(t, 1), :c2] = before
        v_s[i, at(t, 1), c2 : 2 * c2] = x
        v_s[i, at(t, 1), 2 * c2 :] = after

    def window(i, t, count):
        return jnp.concatenate([v_s[i + a, at(t, count), :] for a in range(3)], axis=1)

    def middle(lhs):
        total = jnp.dot(lhs, w_s[...], preferred_element_type=F32)
        return jnp.maximum(total, 0.0).astype(BF16)

    group = 4

    def inner(q, carry):
        t = q * group + 1
        for f in range(group):
            for i in range(height):
                columns(t + f, i + 1, x_ref[q * group + f, i])
        for i in range(1, height - 1):
            m_s[i, at(t, group), :] = middle(window(i, t, group))
        return carry

    lax.fori_loop(0, frames // group, inner, 0)
    arrive()

    def edges(q, carry):
        t = q * group + 1
        for f in range(group):
            for i in (0, height + 1):
                columns(t + f, i, p_s[t + f, i])
        for i in (0, height - 1):
            m_s[i, at(t, group), :] = middle(window(i, t, group))
        return carry

    lax.fori_loop(0, frames // group, edges, 0)

    def outer(q, carry):
        t = q * (frames + 1)
        for i in range(height + 2):
            columns(t, i, p_s[t, i])
        found = middle(jnp.concatenate([window(i, t, 1) for i in range(height)], axis=0))
        for i in range(height):
            m_s[i, at(t, 1), :] = found[i * width : (i + 1) * width]
        return carry

    lax.fori_loop(0, 2, outer, 0)

    def temporal(q, carry):
        for i in range(height):
            total = x_ref[pl.ds(q * group, group), i].astype(F32).reshape(group * width, c2)
            for k in range(3):
                lhs = m_s[i, at(q * group + k, group), :]
                total = total + jnp.dot(lhs, t2_ref[k], preferred_element_type=F32)
            total = jnp.maximum(total, 0.0).astype(BF16)
            out_ref[pl.ds(q * group, group), i] = total.reshape(group, width, c2)
        return carry

    lax.fori_loop(0, frames // group, temporal, 0)


def second(x, mesh, spatial_two, temporal_two):
    frames, height, width, c2 = x.shape
    m2 = spatial_two.shape[2]
    vmem = pl.BlockSpec(memory_space=pltpu.VMEM)
    return pl.pallas_call(
        functools.partial(second_kernel, mesh.shape["tm"], mesh.shape["row"]),
        out_shape=jax.ShapeDtypeStruct((frames, height, width, c2), BF16),
        in_specs=[vmem] * 3,
        out_specs=vmem,
        scratch_shapes=[
            pltpu.VMEM((frames + 2, height + 2, width, c2), BF16),
            pltpu.VMEM((9 * c2, m2), BF16),
            pltpu.VMEM((height + 2, (frames + 2) * width, 3 * c2), BF16),
            pltpu.VMEM((height, (frames + 2) * width, m2), BF16),
            pltpu.SemaphoreType.DMA((len(SIDES),)),
            pltpu.SemaphoreType.DMA((len(SIDES),)),
        ],
        compiler_params=pltpu.CompilerParams(
            collective_id=1, has_side_effects=True, vmem_limit_bytes=48 << 20
        ),
        name="second",
    )(x, spatial_two, temporal_two)


def on_device(mesh, video_clip, spatial_one, temporal_one, down_weight, spatial_two, temporal_two):
    down = jnp.transpose(down_weight, (0, 1, 3, 2))
    one = jnp.transpose(spatial_one, (0, 1, 3, 2))
    temporal = jnp.transpose(temporal_two, (0, 2, 1))
    reduced = first(video_clip, mesh, one, temporal_one, down)
    return second(reduced, mesh, spatial_two, temporal)


def solution(mesh):
    placed = (P("tm", "row", None, None), P(), P(), P(), P(), P())
    return jax.shard_map(
        functools.partial(on_device, mesh),
        mesh=mesh,
        in_specs=placed,
        out_specs=P("tm", "row", None, None),
        check_vma=False,
    )
```
